32 devices in a mesh: parts: 2 (over y), dp: 4 (over x, core), group: 4 (over z).
Axes of the slice: x: 2, y: 2, z: 4, core: 2. Of those that a mesh axis runs over, the one named last changes fastest.
Arguments:
- train_hidden: bfloat16 [256, 64, 14336], P(('parts', 'dp'), None, 'group'), parts along dimension 0, may hold values from -22 to 22
- train_grad: bfloat16 [256, 64, 4096], P(('parts', 'dp'), None, 'group'), parts along dimension 0, may hold values from -8 to 8
- train_mask: int32 [256, 64], P(('parts', 'dp')), parts along dimension 0, may hold values 0 or 1
- syn_hidden: bfloat16 [128, 64, 14336], P(('parts', 'group'), None, 'dp'), parts along dimension 0, may hold values from -22 to 22
- syn_grad: bfloat16 [128, 64, 4096], P(('parts', 'group'), None, 'dp'), parts along dimension 0, may hold values from -8 to 8
- syn_mask: int32 [128, 64], P(('parts', 'group')), parts along dimension 0, may hold values 0 or 1
- basis_in: bfloat16 [14336, 64], replicated, may hold values from -0.046875 to 0.046875
- basis_out: bfloat16 [4096, 64], replicated, may hold values from -0.09375 to 0.09375
Outputs:
- scores: float32 [128, 128], P(('parts', 'group'), 'dp'), parts along dimension 0
The draws below stay inside these ranges and needn't reach their ends.
There are 2 independent parts, one for each index of `parts`. The reference program is written for one: setup_inputs(seed, part) draws one part's arguments, and reference() takes and returns one part's arrays. A program takes and returns all parts, laid end to end along the dimension named above; an argument that names none is the same for every part. Nothing has to cross between parts.
All inputs are finite; a program needn't handle non-finite values. No bound on the sum of `train_mask` or of `syn_mask` on one device may be relied on, other than what follows from the above.
Results may differ from the reference program's by a relative error of at most 0.0003.
Values sent between devices are 32-bit elements; how exact they have to be, the bound alone decides.
A program may use at most 128 MiB of HBM per device.

```python
import math
import jax
import jax.numpy as jnp
from jax import lax

D = 4096
FF = 14336
RANK = 64
LENGTH = 64
TRAIN = 128
SYN = 64


def shared_vector(key, salt, width):
    return jnp.clip(jax.random.normal(jax.random.fold_in(key, salt), (width,), jnp.float32), -4.0, 4.0)


def scaled_rows(key, count):
    logs = jax.random.uniform(key, (count, 1, 1), jnp.float32, math.log(0.3), math.log(3.0))
    return jnp.exp(logs)


def draw_train_hidden(key, part):
    shared = shared_vector(key, 901, FF)
    key = jax.random.fold_in(key, 11)
    base = jnp.clip(jax.random.normal(jax.random.fold_in(key, 1), (TRAIN, LENGTH, FF), jnp.float32), -4.0, 4.0)
    weight = 0.5
    scales = scaled_rows(jax.random.fold_in(key, 2), TRAIN)
    return (scales * (base + weight * shared)).astype(jnp.bfloat16)


def draw_syn_hidden(key, part):
    shared = shared_vector(key, 901, FF)
    key = jax.random.fold_in(key, 12)
    base = jnp.clip(jax.random.normal(jax.random.fold_in(key, 1), (SYN, LENGTH, FF), jnp.float32), -4.0, 4.0)
    weight = 0.5
    scales = scaled_rows(jax.random.fold_in(key, 2), SYN)
    return (scales * (base + weight * shared)).astype(jnp.bfloat16)


def draw_train_grad(key, part):
    shared = shared_vector(key, 902, D)
    key = jax.random.fold_in(key, 13)
    base = jnp.clip(jax.random.normal(jax.random.fold_in(key, 1), (TRAIN, LENGTH, D), jnp.float32), -4.0, 4.0)
    weight = 0.5
    return (base + weight * shared).astype(jnp.bfloat16)


def draw_syn_grad(key, part):
    shared = shared_vector(key, 902, D)
    key = jax.random.fold_in(key, 14)
    base = jnp.clip(jax.random.normal(jax.random.fold_in(key, 1), (SYN, LENGTH, D), jnp.float32), -4.0, 4.0)
    weight = 0.5
    return (base + weight * shared).astype(jnp.bfloat16)


def set_ends(array, rng, smallest, largest):
    place = [jax.random.randint(jax.random.fold_in(rng, axis), (), 0, length) for axis, length in enumerate(array.shape)]
    main_axis = array.shape.index(max(array.shape))
    neighbour = place[:main_axis] + [(place[main_axis] + 1) % array.shape[main_axis]] + place[main_axis + 1:]
    return array.at[tuple(place)].set(smallest).at[tuple(neighbour)].set(largest)


def noise(rng, shape, deviation, limit, held_as=jnp.bfloat16):
    array = deviation * jax.random.normal(rng, shape, jnp.float32)
    return jnp.clip(array, min=-limit, max=limit).astype(held_as)


def setup_inputs(seed: int = 0, part: int = 0) -> dict:
    splits = jax.random.split(jax.random.key(seed), 9)
    own_keys = jax.random.split(jax.random.fold_in(splits[8], part), 9)
    return {
        "train_hidden": draw_train_hidden(jax.random.fold_in(jax.random.fold_in(splits[8], part), 71), part),
        "train_grad": draw_train_grad(jax.random.fold_in(jax.random.fold_in(splits[8], part), 71), part),
        "train_mask": set_ends((jax.random.randint(own_keys[2], (TRAIN, LENGTH), 0, 4) < 3).astype(jnp.int32), jax.random.fold_in(own_keys[2], 1), 0, 1),
        "syn_hidden": draw_syn_hidden(jax.random.fold_in(jax.random.fold_in(splits[8], part), 71), part),
        "syn_grad": draw_syn_grad(jax.random.fold_in(jax.random.fold_in(splits[8], part), 71), part),
        "syn_mask": set_ends((jax.random.randint(own_keys[5], (SYN, LENGTH), 0, 4) < 3).astype(jnp.int32), jax.random.fold_in(own_keys[5], 1), 0, 1),
        "basis_in": noise(splits[6], (FF, RANK), FF ** -0.5, 0.046875),
        "basis_out": noise(splits[7], (D, RANK), D ** -0.5, 0.09375),
    }


damp_ratio = 0.1

def projections(hidden, grads, basis_in, basis_out):
    seqs, length, width = hidden.shape
    in_proj = jnp.dot(hidden.reshape(seqs * length, width).astype(jnp.float32), basis_in.astype(jnp.float32), preferred_element_type=jnp.float32)
    out_proj = jnp.dot(grads.reshape(seqs * length, grads.shape[2]).astype(jnp.float32), basis_out.astype(jnp.float32), preferred_element_type=jnp.float32)
    return (in_proj.reshape(seqs, length, -1), out_proj.reshape(seqs, length, -1))

def make_codes(in_proj, out_proj, mask):
    weighted = out_proj * mask[:, :, None].astype(jnp.float32)
    codes = jnp.einsum('nta,ntb->nab', weighted, in_proj, precision=lax.Precision.HIGHEST)
    return codes.reshape(codes.shape[0], -1)

def reference(train_hidden, train_grad, train_mask, syn_hidden, syn_grad, syn_mask, basis_in, basis_out):
    in_proj, out_proj = projections(train_hidden, train_grad, basis_in, basis_out)
    codes = make_codes(in_proj, out_proj, train_mask)
    syn_in, syn_out = projections(syn_hidden, syn_grad, basis_in, basis_out)
    syn_codes = make_codes(syn_in, syn_out, syn_mask)
    gram = jnp.dot(codes, codes.T, precision=lax.Precision.HIGHEST)
    damp = damp_ratio * jnp.trace(gram) / gram.shape[0]
    system = gram + damp * jnp.eye(gram.shape[0], dtype=jnp.float32)
    lower = jnp.linalg.cholesky(system)
    raw = jnp.dot(syn_codes, codes.T, precision=lax.Precision.HIGHEST)
    first = lax.linalg.triangular_solve(lower, raw.T, left_side=True, lower=True)
    solved = lax.linalg.triangular_solve(lower, first, left_side=True, lower=True, transpose_a=True)
    return solved.T
```

```python
import functools

import jax
import jax.numpy as jnp
from jax import lax
from jax.experimental import pallas as pl
from jax.experimental.pallas import tpu as pltpu
from jax.sharding import PartitionSpec as P

damp_ratio = 0.1


def local_terms(hidden, grads, basis_in, basis_out, index):
    seqs, length, width = hidden.shape
    feat = grads.shape[2]
    in_rows = lax.dynamic_slice_in_dim(basis_in, index * width, width, 0)
    out_rows = lax.dynamic_slice_in_dim(basis_out, index * feat, feat, 0)
    in_proj = jnp.dot(
        hidden.reshape(seqs * length, width), in_rows, preferred_element_type=jnp.float32
    )
    out_proj = jnp.dot(
        grads.reshape(seqs * length, feat), out_rows, preferred_element_type=jnp.float32
    )
    return jnp.concatenate([in_proj, out_proj], axis=1).reshape(seqs, length, -1)


def make_codes(stacked, mask, rank):
    in_proj = stacked[:, :, :rank]
    weighted = stacked[:, :, rank:] * mask[:, :, None].astype(jnp.float32)
    codes = jnp.einsum("nta,ntb->nab", weighted, in_proj, precision=lax.Precision.HIGHEST)
    return codes.reshape(codes.shape[0], -1)


def body(train_hidden, train_grad, train_mask, syn_hidden, syn_grad, syn_mask, basis_in, basis_out):
    rank = basis_in.shape[1]
    group_pos = lax.axis_index("group")
    data_pos = lax.axis_index("dp")
    train_terms = local_terms(train_hidden, train_grad, basis_in, basis_out, group_pos)
    summed = lax.psum(train_terms, "group")
    codes = make_codes(summed, train_mask, rank)
    syn_terms = local_terms(syn_hidden, syn_grad, basis_in, basis_out, data_pos)
    syn_summed = lax.psum(syn_terms, "dp")
    syn_codes = make_codes(syn_summed, syn_mask, rank)
    width = rank * rank // lax.axis_size("group")
    columns = lax.dynamic_slice_in_dim(codes, group_pos * width, width, 1)
    every = lax.all_gather(columns, "dp", axis=0, tiled=True)
    partial_value = jnp.dot(every, every.T, precision=lax.Precision.HIGHEST)
    gram = lax.psum(partial_value, "group")
    total = gram.shape[0]
    local_count = codes.shape[0]
    damp = damp_ratio * jnp.trace(gram) / total
    system = gram + damp * jnp.eye(total, dtype=jnp.float32)
    lower = jnp.linalg.cholesky(system)
    row_ids = lax.broadcasted_iota(jnp.int32, (total, local_count), 0)
    col_ids = lax.broadcasted_iota(jnp.int32, (total, local_count), 1) + data_pos * local_count
    unit_cols = (row_ids == col_ids).astype(jnp.float32)
    first = lax.linalg.triangular_solve(lower, unit_cols, left_side=True, lower=True)
    inverse_cols = lax.linalg.triangular_solve(
        lower, first, left_side=True, lower=True, transpose_a=True
    )
    raw = jnp.dot(syn_codes, codes.T, precision=lax.Precision.HIGHEST)
    initial = jnp.zeros((raw.shape[0], local_count), jnp.float32)
    return initial + jnp.dot(
        lax.all_gather(raw, "dp", axis=1, tiled=True), inverse_cols, precision=lax.Precision.HIGHEST
    )


MESH = pl.DeviceIdType.MESH
HIGHEST = lax.Precision.HIGHEST


def mm(a, b, contract=((1,), (0,))):
    return lax.dot_general(
        a, b, (contract, ((), ())), precision=HIGHEST, preferred_element_type=jnp.float32
    )


def inverse(system, bound):
    total = system.shape[0]
    rows = lax.broadcasted_iota(jnp.int32, (total, total), 0)
    cols = lax.broadcasted_iota(jnp.int32, (total, total), 1)
    eye = (rows == cols).astype(jnp.float32)
    trace = jnp.sum(jnp.sum(system * eye, axis=1, keepdims=True), axis=0, keepdims=True)
    damp = trace * (damp_ratio / total)
    system = system + damp * eye
    scale = 2.0 / (trace + 2.0 * damp)
    error = eye - scale * system
    value = scale * eye
    radius = (bound - 1.0) / (bound + 1.0)
    while radius > 3e-6:
        step = 2.0 / (2.0 - radius * radius)
        both = mm(jnp.concatenate([error, value], axis=0), error)
        value = step * (value + both[total:])
        error = step * both[:total] - (step - 1.0) * eye
        radius = radius * radius / (2.0 - radius * radius)
    return system, value


def kernel(
    dims, th, tg, tm, sh, sg, sm, bi, bo, out,
    th_v, tg_v, sh_v, sg_v, bi_v, bo_v, ci_v, co_v, wi_v, wo_v, vi_v, vo_v,
    zs, zr, xs, xr, cs, cr, ps, pr, fs, fr,
    load_sem, z_send, z_recv, x_send, x_recv, c_send, c_recv, p_send, p_recv, f_send, f_recv,
):
    D, G, T, S, L, rank = dims
    N = D * G
    half = rank // 2
    per = half // N
    d = lax.axis_index("dp")
    g = lax.axis_index("group")
    me = d * G + g

    def peer(step):
        j = lax.rem(me + step, N)
        return j, {"dp": lax.div(j, G), "group": lax.rem(j, G)}

    def load(src, dst, index):
        return pltpu.make_async_copy(src, dst, load_sem.at[index])

    def rows_of(ref, place, count):
        return ref.at[pl.ds(pl.multiple_of(place * count, count), count)]

    basis_loads = [
        load(rows_of(bi, g, th.shape[1]), bi_v, 0),
        load(rows_of(bo, g, tg.shape[1]), bo_v, 1),
        load(rows_of(bi, d, sh.shape[1]), ci_v, 2),
        load(rows_of(bo, d, sg.shape[1]), co_v, 3),
    ]
    order = [("t", s) for s in range(1, G)] + [("s", s) for s in range(1, D)] + [("t", 0), ("s", 0)]
    loads = []
    for i, (kind, s) in enumerate(order):
        if kind == "t":
            place = lax.rem(g + s, G)
            pair = (load(rows_of(th, place, T * L), th_v.at[s], 4 + 2 * i),
                    load(rows_of(tg, place, T * L), tg_v.at[s], 5 + 2 * i))
        else:
            place = lax.rem(d + s, D)
            pair = (load(rows_of(sh, place, S * L), sh_v.at[s], 4 + 2 * i),
                    load(rows_of(sg, place, S * L), sg_v.at[s], 5 + 2 * i))
        loads.append(pair)

    def start(i):
        if i < len(loads):
            loads[i][0].start()
            loads[i][1].start()

    depth = 3
    basis_loads[0].start()
    basis_loads[1].start()
    for i in range(depth):
        start(i)
        if i == 0:
            basis_loads[2].start()
            basis_loads[3].start()

    barrier = pltpu.get_barrier_semaphore()

    def greet(step, carry):
        pl.semaphore_signal(barrier, inc=1, device_id=peer(step)[1], device_id_type=MESH)
        return carry

    lax.fori_loop(1, N, greet, 0)
    cs[:, T:, :] = jnp.zeros((half, cs.shape[1] - T, 2 * rank), jnp.float32)

    def pad(raw, wide, first):
        value = raw[...]
        blank = jnp.zeros_like(value)
        wide[...] = jnp.concatenate([value, blank] if first else [blank, value], axis=1)

    basis_loads[0].wait()
    pad(bi_v, wi_v, True)
    basis_loads[1].wait()
    pad(bo_v, wo_v, False)
    sends = []
    for i, (kind, s) in enumerate(order):
        loads[i][0].wait()
        loads[i][1].wait()
        start(i + depth)
        if kind == "s" and s == min(1, D - 1):
            basis_loads[2].wait()
            pad(ci_v, vi_v, True)
            basis_loads[3].wait()
            pad(co_v, vo_v, False)
        if kind == "t":
            zs[s] = jnp.dot(th_v[s], wi_v[...], preferred_element_type=jnp.float32) + jnp.dot(
                tg_v[s], wo_v[...], preferred_element_type=jnp.float32)
        else:
            xs[s] = jnp.dot(sh_v[s], vi_v[...], preferred_element_type=jnp.float32) + jnp.dot(
                sg_v[s], vo_v[...], preferred_element_type=jnp.float32)
        if i == 0:
            pl.semaphore_wait(barrier, N - 1)
        if s > 0:
            if kind == "t":
                copy = pltpu.make_async_remote_copy(
                    src_ref=zs.at[s], dst_ref=zr.at[s], send_sem=z_send.at[s], recv_sem=z_recv.at[s],
                    device_id={"group": lax.rem(g + s, G)}, device_id_type=MESH)
            else:
                copy = pltpu.make_async_remote_copy(
                    src_ref=xs.at[s], dst_ref=xr.at[s], send_sem=x_send.at[s], recv_sem=x_recv.at[s],
                    device_id={"dp": lax.rem(d + s, D)}, device_id_type=MESH)
            copy.start()
            sends.append((kind, copy))

    def codes(kind, own, received, mask, count, peers, place, first):
        for k, copy in sends:
            if k == kind:
                copy.wait_recv()
        for n in range(count):
            rows = pl.ds(n * L, L)
            total = own[0, rows, :]
            for s in range(1, peers):
                total = total + received[s, rows, :]
            turned = total.T
            keep = mask[pl.ds(place * count + n, 1), :].astype(jnp.float32)
            code = mm(turned[rank:] * keep, total[:, :rank])
            cs[:, first + n, :] = jnp.concatenate([code[:half], code[half:]], axis=1)

    codes("s", xs, xr, sm, S, D, d, T)
    codes("t", zs, zr, tm, T, G, g, 0)

    def exchange(source, landing, send_sem, recv_sem):
        def copy(step, slot):
            j, where = peer(step)
            return pltpu.make_async_remote_copy(
                src_ref=source(j), dst_ref=landing.at[slot], send_sem=send_sem.at[step],
                recv_sem=recv_sem.at[slot], device_id=where, device_id_type=MESH)

        def send(step, carry):
            copy(step, me).start()
            return carry

        def arrive(step, carry):
            copy(step, lax.rem(me + N - step, N)).wait_recv()
            return carry

        def left(step, carry):
            copy(step, me).wait_send()
            return carry

        lax.fori_loop(1, N, send, 0)
        yield
        lax.fori_loop(1, N, arrive, 0)
        yield
        lax.fori_loop(1, N, left, 0)
        yield

    R = cs.shape[1]
    swap = exchange(lambda j: cs.at[pl.ds(j * per, per)], cr, c_send, c_recv)
    next(swap)
    cr[me] = cs[pl.ds(me * per, per)]
    next(swap)
    train = jnp.concatenate([cr[:, p, :T, :].reshape(N * T, 2 * rank) for p in range(per)], axis=1)
    syn = jnp.concatenate([cr[:, p, T:, :].reshape(N * (R - T), 2 * rank) for p in range(per)], axis=1)
    product = mm(jnp.concatenate([train, syn], axis=0), train, ((1,), (1,)))
    ps[:, :T, :] = product[: N * T].reshape(N, T, N * T)
    ps[:, T:, :] = product[N * T :].reshape(N, R - T, N * T)
    reduce = exchange(lambda j: ps.at[j], pr, p_send, p_recv)
    next(reduce)
    pr[me] = ps[me]
    next(reduce)
    mine = pr[0]
    for j in range(1, N):
        mine = mine + pr[j]
    fs[...] = mine
    gather = exchange(lambda j: fs, fr, f_send, f_recv)
    next(gather)
    fr[me] = mine
    next(gather)
    gram = fr[:, :T, :].reshape(N * T, N * T)
    raw = jnp.concatenate([fr[p * G + g, T:, :] for p in range(D)], axis=0)
    system, value = inverse(gram, 1.0 + N * T / damp_ratio)
    scores = mm(raw, value)
    scores = scores + mm(raw - mm(scores, system), value)
    for p in range(D):
        out[pl.ds(p * S, S), :] = scores[p * (R - T) : p * (R - T) + S]
    for k, copy in sends:
        copy.wait_send()
    next(swap)
    next(reduce)
    next(gather)


def fused(D, G, th, tg, tm, sh, sg, sm, bi, bo):
    rank = bi.shape[1]
    L = th.shape[1]
    T, S = th.shape[0] // G, sh.shape[0] // D
    N = D * G
    R = T + 8 * ((S + 7) // 8)
    total = N * T
    per = rank // 2 // N
    f32, bf16 = jnp.float32, jnp.bfloat16
    flat = lambda x: x.reshape(x.shape[0] * x.shape[1], x.shape[2])
    ins, outs, sins, souts = th.shape[2], tg.shape[2], sh.shape[2], sg.shape[2]
    dma = lambda n: pltpu.SemaphoreType.DMA((n,))
    anywhere = pl.BlockSpec(memory_space=pl.ANY)
    local = pl.BlockSpec(memory_space=pltpu.VMEM)
    scores = pl.pallas_call(
        functools.partial(kernel, (D, G, T, S, L, rank)),
        out_shape=jax.ShapeDtypeStruct((D * S, total), f32),
        in_specs=[anywhere, anywhere, local, anywhere, anywhere, local, anywhere, anywhere],
        out_specs=local,
        scratch_shapes=[
            pltpu.VMEM((G, T * L, ins), bf16), pltpu.VMEM((G, T * L, outs), bf16),
            pltpu.VMEM((D, S * L, sins), bf16), pltpu.VMEM((D, S * L, souts), bf16),
            pltpu.VMEM((ins, rank), bf16), pltpu.VMEM((outs, rank), bf16),
            pltpu.VMEM((sins, rank), bf16), pltpu.VMEM((souts, rank), bf16),
            pltpu.VMEM((ins, 2 * rank), bf16), pltpu.VMEM((outs, 2 * rank), bf16),
            pltpu.VMEM((sins, 2 * rank), bf16), pltpu.VMEM((souts, 2 * rank), bf16),
            pltpu.VMEM((G, T * L, 2 * rank), f32), pltpu.VMEM((G, T * L, 2 * rank), f32),
            pltpu.VMEM((D, S * L, 2 * rank), f32), pltpu.VMEM((D, S * L, 2 * rank), f32),
            pltpu.VMEM((rank // 2, R, 2 * rank), f32), pltpu.VMEM((N, per, R, 2 * rank), f32),
            pltpu.VMEM((N, R, total), f32), pltpu.VMEM((N, R, total), f32),
            pltpu.VMEM((R, total), f32), pltpu.VMEM((N, R, total), f32),
            dma(4 + 2 * (G + D)), dma(G), dma(G), dma(D), dma(D),
            dma(N), dma(N), dma(N), dma(N), dma(N), dma(N),
        ],
        compiler_params=pltpu.CompilerParams(
            collective_id=0, has_side_effects=True, vmem_limit_bytes=56 * 1024 * 1024
        ),
        cost_estimate=pl.CostEstimate(flops=2 * 10**9, bytes_accessed=30 * 10**6, transcendentals=0),
    )(flat(th), flat(tg), tm, flat(sh), flat(sg), sm, bi, bo)
    width = total // D
    return lax.dynamic_slice_in_dim(scores, lax.axis_index("dp") * width, width, 1)


def fits(D, G, train, syn, rank):
    N = D * G
    return (
        train % (8 * N) == 0 and train // N == 8 and syn % N == 0 and syn // N <= 8
        and rank == 64 and (rank // 2) % N == 0
    )


def solution(mesh):
    placed = (
        P(("parts", "dp"), None, "group"),
        P(("parts", "dp"), None, "group"),
        P(("parts", "dp"), None),
        P(("parts", "group"), None, "dp"),
        P(("parts", "group"), None, "dp"),
        P(("parts", "group"), None),
        P(),
        P(),
    )
    D, G = mesh.shape["dp"], mesh.shape["group"]

    def local(*args):
        train, syn, rank = args[0].shape[0] * D, args[3].shape[0] * G, args[6].shape[1]
        if fits(D, G, train, syn, rank):
            return fused(D, G, *args)
        return body(*args)

    return jax.shard_map(
        local, mesh=mesh, in_specs=placed, out_specs=P(("parts", "group"), "dp"), check_vma=False
    )
```

```python
import functools

import jax
import jax.numpy as jnp
from jax import lax
from jax.experimental import pallas as pl
from jax.experimental.pallas import tpu as pltpu
from jax.sharding import PartitionSpec as P

damp_ratio = 0.1


def local_terms(hidden, grads, basis_in, basis_out, index):
    seqs, length, width = hidden.shape
    feat = grads.shape[2]
    in_rows = lax.dynamic_slice_in_dim(basis_in, index * width, width, 0)
    out_rows = lax.dynamic_slice_in_dim(basis_out, index * feat, feat, 0)
    in_proj = jnp.dot(
        hidden.reshape(seqs * length, width), in_rows, preferred_element_type=jnp.float32
    )
    out_proj = jnp.dot(
        grads.reshape(seqs * length, feat), out_rows, preferred_element_type=jnp.float32
    )
    return jnp.concatenate([in_proj, out_proj], axis=1).reshape(seqs, length, -1)


def make_codes(stacked, mask, rank):
    in_proj = stacked[:, :, :rank]
    weighted = stacked[:, :, rank:] * mask[:, :, None].astype(jnp.float32)
    codes = jnp.einsum("nta,ntb->nab", weighted, in_proj, precision=lax.Precision.HIGHEST)
    return codes.reshape(codes.shape[0], -1)


def body(train_hidden, train_grad, train_mask, syn_hidden, syn_grad, syn_mask, basis_in, basis_out):
    rank = basis_in.shape[1]
    group_pos = lax.axis_index("group")
    data_pos = lax.axis_index("dp")
    train_terms = local_terms(train_hidden, train_grad, basis_in, basis_out, group_pos)
    summed = lax.psum(train_terms, "group")
    codes = make_codes(summed, train_mask, rank)
    syn_terms = local_terms(syn_hidden, syn_grad, basis_in, basis_out, data_pos)
    syn_summed = lax.psum(syn_terms, "dp")
    syn_codes = make_codes(syn_summed, syn_mask, rank)
    width = rank * rank // lax.axis_size("group")
    columns = lax.dynamic_slice_in_dim(codes, group_pos * width, width, 1)
    every = lax.all_gather(columns, "dp", axis=0, tiled=True)
    partial_value = jnp.dot(every, every.T, precision=lax.Precision.HIGHEST)
    gram = lax.psum(partial_value, "group")
    total = gram.shape[0]
    local_count = codes.shape[0]
    damp = damp_ratio * jnp.trace(gram) / total
    system = gram + damp * jnp.eye(total, dtype=jnp.float32)
    lower = jnp.linalg.cholesky(system)
    row_ids = lax.broadcasted_iota(jnp.int32, (total, local_count), 0)
    col_ids = lax.broadcasted_iota(jnp.int32, (total, local_count), 1) + data_pos * local_count
    unit_cols = (row_ids == col_ids).astype(jnp.float32)
    first = lax.linalg.triangular_solve(lower, unit_cols, left_side=True, lower=True)
    inverse_cols = lax.linalg.triangular_solve(
        lower, first, left_side=True, lower=True, transpose_a=True
    )
    raw = jnp.dot(syn_codes, codes.T, precision=lax.Precision.HIGHEST)
    initial = jnp.zeros((raw.shape[0], local_count), jnp.float32)
    return initial + jnp.dot(
        lax.all_gather(raw, "dp", axis=1, tiled=True), inverse_cols, precision=lax.Precision.HIGHEST
    )


MESH = pl.DeviceIdType.MESH
HIGHEST = lax.Precision.HIGHEST


def mm(a, b, contract=((1,), (0,))):
    return lax.dot_general(
        a, b, (contract, ((), ())), precision=HIGHEST, preferred_element_type=jnp.float32
    )


def inverse(system, bound):
    total = system.shape[0]
    rows = lax.broadcasted_iota(jnp.int32, (total, total), 0)
    cols = lax.broadcasted_iota(jnp.int32, (total, total), 1)
    eye = (rows == cols).astype(jnp.float32)
    trace = jnp.sum(jnp.sum(system * eye, axis=1, keepdims=True), axis=0, keepdims=True)
    damp = trace * (damp_ratio / total)
    system = system + damp * eye
    scale = 2.0 / (trace + 2.0 * damp)
    error = eye - scale * system
    value = scale * eye
    radius = (bound - 1.0) / (bound + 1.0)
    while radius > 3e-6:
        step = 2.0 / (2.0 - radius * radius)
        both = mm(jnp.concatenate([error, value], axis=0), error)
        value = step * (value + both[total:])
        error = step * both[:total] - (step - 1.0) * eye
        radius = radius * radius / (2.0 - radius * radius)
    return system, value


def kernel(
    dims, th, tg, tm, sh, sg, sm, bi, bo, out,
    th_v, tg_v, sh_v, sg_v, bi_v, bo_v, ci_v, co_v,
    zs, zr, xs, xr, cs, cr, ps, pr, fs, fr,
    load_sem, z_send, z_recv, x_send, x_recv, c_send, c_recv, p_send, p_recv, f_send, f_recv,
):
    D, G, T, S, L, rank = dims
    N = D * G
    half = rank // 2
    per = half // N
    d = lax.axis_index("dp")
    g = lax.axis_index("group")
    me = d * G + g

    def peer(step):
        j = lax.rem(me + step, N)
        return j, {"dp": lax.div(j, G), "group": lax.rem(j, G)}

    def load(src, dst, index):
        return pltpu.make_async_copy(src, dst, load_sem.at[index])

    def rows_of(ref, place, count):
        return ref.at[pl.ds(pl.multiple_of(place * count, count), count)]

    def columns_of(ref, place, count):
        return ref.at[:, pl.ds(pl.multiple_of(place * count, count), count)]

    low = 2 * g < G

    def target(i):
        near = jnp.where(low, g, G - 1 - g)
        far = G - 1 - near
        place = near if i == G - 1 else jnp.where(i < far, G - 1 - i, i - far)
        return jnp.where(low, place, G - 1 - place)

    basis_loads = [
        load(columns_of(bi, g, th.shape[1]), bi_v, 0),
        load(columns_of(bo, g, tg.shape[1]), bo_v, 1),
        load(columns_of(bi, d, sh.shape[1]), ci_v, 2),
        load(columns_of(bo, d, sg.shape[1]), co_v, 3),
    ]
    targets = [target(i) for i in range(G)]
    order = [("t", i) for i in range(G)] + [("s", s) for s in range(1, D)] + [("s", 0)]
    loads = []
    for i, (kind, s) in enumerate(order):
        if kind == "t":
            place = targets[s]
            pair = (load(rows_of(th, place, T * L), th_v.at[s], 4 + 2 * i),
                    load(rows_of(tg, place, T * L), tg_v.at[s], 5 + 2 * i))
        else:
            place = lax.rem(d + s, D)
            pair = (load(rows_of(sh, place, S * L), sh_v.at[s], 4 + 2 * i),
                    load(rows_of(sg, place, S * L), sg_v.at[s], 5 + 2 * i))
        loads.append(pair)

    def start(i):
        if i < len(loads):
            loads[i][0].start()
            loads[i][1].start()

    depth = 3
    basis_loads[0].start()
    basis_loads[1].start()
    for i in range(depth):
        start(i)
        if i == 0:
            basis_loads[2].start()
            basis_loads[3].start()

    barrier = pltpu.get_barrier_semaphore()

    def greet(step, carry):
        pl.semaphore_signal(barrier, inc=1, device_id=peer(step)[1], device_id_type=MESH)
        return carry

    lax.fori_loop(1, N, greet, 0)

    def project(basis, chunk):
        return lax.dot_general(
            basis, chunk, (((1,), (1,)), ((), ())), preferred_element_type=jnp.float32)

    edge = (g == 0) | (g == G - 1)

    def onward(t):
        right = t > g
        slot = jnp.where(right | (t != g - 1), t, G)
        return pltpu.make_async_remote_copy(
            src_ref=zs.at[t], dst_ref=zr.at[slot], send_sem=z_send.at[t], recv_sem=z_recv.at[slot],
            device_id={"group": jnp.where(right, jnp.minimum(g + 1, G - 1), jnp.maximum(g - 1, 0))},
            device_id_type=MESH)

    def landed(slot):
        pltpu.make_async_remote_copy(
            src_ref=zs.at[0], dst_ref=zr.at[slot], send_sem=z_send.at[0], recv_sem=z_recv.at[slot],
            device_id={"group": jnp.where(g > 0, g - 1, g + 1)}, device_id_type=MESH).wait_recv()

    def forward(i):
        t = targets[i]

        @pl.when(jnp.logical_not(edge))
        def _():
            landed(t)
            zs[t] = zs[t] + zr[t]
            onward(t).start()

    basis_loads[0].wait()
    basis_loads[1].wait()
    sends = []
    for i, (kind, s) in enumerate(order):
        loads[i][0].wait()
        loads[i][1].wait()
        start(i + depth)
        if kind == "t":
            t = targets[s]
            zs[t, :rank] = project(bi_v[...], th_v[s])
            zs[t, rank:] = project(bo_v[...], tg_v[s])
            if i == 0:
                pl.semaphore_wait(barrier, N - 1)
            if s < G - 1:
                pl.when(edge)(lambda: onward(t).start())
        else:
            if i == G:
                basis_loads[2].wait()
                basis_loads[3].wait()
                forward(0)
            xs[s, :rank] = project(ci_v[...], sh_v[s])
            xs[s, rank:] = project(co_v[...], sg_v[s])
            if s > 0:
                copy = pltpu.make_async_remote_copy(
                    src_ref=xs.at[s], dst_ref=xr.at[s], send_sem=x_send.at[s], recv_sem=x_recv.at[s],
                    device_id={"dp": lax.rem(d + s, D)}, device_id_type=MESH)
                copy.start()
                sends.append(copy)

    def codes(total, mask, count, place, first):
        lanes = lax.broadcasted_iota(jnp.int32, (1, 2 * L), 1)
        for n in range(0, count, 2):
            both = total(pl.ds(n * L, 2 * L))
            keep = jnp.concatenate(
                [mask[pl.ds(place * count + n, 1), :], mask[pl.ds(place * count + n + 1, 1), :]], axis=1
            ).astype(jnp.float32)
            left = jnp.where(lanes < L, keep, 0.0)
            right = jnp.where(lanes < L, 0.0, keep)
            weighted = jnp.concatenate([both[rank:] * left, both[rank:] * right], axis=0)
            pair = mm(weighted, both[:rank], ((1,), (1,)))
            for k in range(2):
                code = pair[k * rank : (k + 1) * rank]
                cs[:, first + n + k, :] = jnp.concatenate([code[:half], code[half:]], axis=1)

    for i in range(1, G - 1):
        forward(i)
    for copy in sends:
        copy.wait_recv()
    codes(lambda c: sum((xr[s, :, c] for s in range(1, D)), xs[0, :, c]), sm, S, d, T)

    @pl.when(g > 0)
    def _():
        landed(g)
        zs[g] = zs[g] + zr[g]

    @pl.when(g < G - 1)
    def _():
        landed(G)
        zs[g] = zs[g] + zr[G]

    codes(lambda c: zs[g, :, c], tm, T, g, 0)

    def exchange(source, landing, send_sem, recv_sem):
        def copy(step, slot):
            j, where = peer(step)
            return pltpu.make_async_remote_copy(
                src_ref=source(j), dst_ref=landing.at[slot], send_sem=send_sem.at[step],
                recv_sem=recv_sem.at[slot], device_id=where, device_id_type=MESH)

        def send(step, carry):
            copy(step, me).start()
            return carry

        def arrive(step, carry):
            copy(step, lax.rem(me + N - step, N)).wait_recv()
            return carry

        def left(step, carry):
            copy(step, me).wait_send()
            return carry

        lax.fori_loop(1, N, send, 0)
        yield
        lax.fori_loop(1, N, arrive, 0)
        yield
        lax.fori_loop(1, N, left, 0)
        yield

    R = cs.shape[1]
    swap = exchange(lambda j: cs.at[pl.ds(j * per, per)], cr, c_send, c_recv)
    next(swap)
    cr[me] = cs[pl.ds(me * per, per)]
    next(swap)
    train = jnp.concatenate([cr[:, p, :T, :].reshape(N * T, 2 * rank) for p in range(per)], axis=1)
    syn = jnp.concatenate([cr[:, p, T:, :].reshape(N * (R - T), 2 * rank) for p in range(per)], axis=1)
    product = mm(jnp.concatenate([train, syn], axis=0), train, ((1,), (1,)))
    ps[:, :T, :] = product[: N * T].reshape(N, T, N * T)
    ps[:, T:, :] = product[N * T :].reshape(N, R - T, N * T)
    reduce = exchange(lambda j: ps.at[j], pr, p_send, p_recv)
    next(reduce)
    pr[me] = ps[me]
    next(reduce)
    mine = pr[0]
    for j in range(1, N):
        mine = mine + pr[j]
    fs[...] = mine
    gather = exchange(lambda j: fs, fr, f_send, f_recv)
    next(gather)
    fr[me] = mine
    next(gather)
    gram = fr[:, :T, :].reshape(N * T, N * T)
    raw = jnp.concatenate([fr[p * G + g, T:, :] for p in range(D)], axis=0)
    system, value = inverse(gram, 1.0 + N * T / damp_ratio)
    scores = mm(raw, value)
    scores = scores + mm(raw - mm(scores, system), value)
    width = out.shape[1]
    chosen = scores[:, :width]
    for p in range(1, D):
        chosen = jnp.where(d == p, scores[:, p * width : (p + 1) * width], chosen)
    out[...] = chosen
    for copy in sends:
        copy.wait_send()
    for i in range(G - 1):
        onward(targets[i]).wait_send()
    next(swap)
    next(reduce)
    next(gather)


def fused(D, G, th, tg, tm, sh, sg, sm, bi, bo):
    rank = bi.shape[1]
    L = th.shape[1]
    T, S = th.shape[0] // G, sh.shape[0] // D
    N = D * G
    R = T + S
    total = N * T
    per = rank // 2 // N
    f32, bf16 = jnp.float32, jnp.bfloat16
    flat = lambda x: x.reshape(x.shape[0] * x.shape[1], x.shape[2])
    ins, outs, sins, souts = th.shape[2], tg.shape[2], sh.shape[2], sg.shape[2]
    dma = lambda n: pltpu.SemaphoreType.DMA((n,))
    anywhere = pl.BlockSpec(memory_space=pl.ANY)
    local = pl.BlockSpec(memory_space=pltpu.VMEM)
    return pl.pallas_call(
        functools.partial(kernel, (D, G, T, S, L, rank)),
        out_shape=jax.ShapeDtypeStruct((D * S, total // D), f32),
        in_specs=[anywhere, anywhere, local, anywhere, anywhere, local, anywhere, anywhere],
        out_specs=local,
        scratch_shapes=[
            pltpu.VMEM((G, T * L, ins), bf16), pltpu.VMEM((G, T * L, outs), bf16),
            pltpu.VMEM((D, S * L, sins), bf16), pltpu.VMEM((D, S * L, souts), bf16),
            pltpu.VMEM((rank, ins), bf16), pltpu.VMEM((rank, outs), bf16),
            pltpu.VMEM((rank, sins), bf16), pltpu.VMEM((rank, souts), bf16),
            pltpu.VMEM((G, 2 * rank, T * L), f32), pltpu.VMEM((G + 1, 2 * rank, T * L), f32),
            pltpu.VMEM((D, 2 * rank, S * L), f32), pltpu.VMEM((D, 2 * rank, S * L), f32),
            pltpu.VMEM((rank // 2, R, 2 * rank), f32), pltpu.VMEM((N, per, R, 2 * rank), f32),
            pltpu.VMEM((N, R, total), f32), pltpu.VMEM((N, R, total), f32),
            pltpu.VMEM((R, total), f32), pltpu.VMEM((N, R, total), f32),
            dma(4 + 2 * (G + D)), dma(G), dma(G + 1), dma(D), dma(D),
            dma(N), dma(N), dma(N), dma(N), dma(N), dma(N),
        ],
        compiler_params=pltpu.CompilerParams(
            collective_id=0, has_side_effects=True, vmem_limit_bytes=56 * 1024 * 1024
        ),
        cost_estimate=pl.CostEstimate(flops=2 * 10**9, bytes_accessed=30 * 10**6, transcendentals=0),
    )(flat(th), flat(tg), tm, flat(sh), flat(sg), sm, bi.T, bo.T)


def fits(D, G, train, syn, rank):
    N = D * G
    return (
        train % (8 * N) == 0 and train // N == 8 and syn % N == 0 and syn // N <= 8
        and syn // N % 2 == 0 and G > 1 and D > 1 and 2 * rank % 128 == 0 and (rank // 2) % N == 0
    )


def solution(mesh):
    placed = (
        P(("parts", "dp"), None, "group"),
        P(("parts", "dp"), None, "group"),
        P(("parts", "dp"), None),
        P(("parts", "group"), None, "dp"),
        P(("parts", "group"), None, "dp"),
        P(("parts", "group"), None),
        P(),
        P(),
    )
    D, G = mesh.shape["dp"], mesh.shape["group"]

    def local(*args):
        train, syn, rank = args[0].shape[0] * D, args[3].shape[0] * G, args[6].shape[1]
        if fits(D, G, train, syn, rank):
            return fused(D, G, *args)
        return body(*args)

    return jax.shard_map(
        local, mesh=mesh, in_specs=placed, out_specs=P(("parts", "group"), "dp"), check_vma=False
    )
```
